32 devices in a mesh: groups: 2 (over y), rows: 4 (over z), shard: 4 (over x, core).
Axes of the slice: x: 2, y: 2, z: 4, core: 2. Of those that a mesh axis runs over, the one named last changes fastest.
Arguments:
- images: bfloat16 [8, 8, 128, 512], P(('groups', 'shard'), 'rows'), parts along dimension 0, may hold values from -6 to 6
- cotangent: bfloat16 [8, 8, 128, 512], P(('groups', 'shard'), 'rows'), parts along dimension 0, may hold values from -6 to 6
- weight_in: bfloat16 [2, 512, 512], P(None, 'shard'), may hold values from -0.25 to 0.25
- weight_group: bfloat16 [2, 144, 512], P(None, 'shard'), may hold values from -0.5 to 0.5
- weight_out: bfloat16 [2, 512, 512], P(None, 'shard'), may hold values from -0.25 to 0.25
Outputs:
- decoded: bfloat16 [8, 8, 128, 512], P(('groups', 'shard'), 'rows'), parts along dimension 0
- grad_images: bfloat16 [8, 8, 128, 512], P(('groups', 'shard'), 'rows'), parts along dimension 0
- grad_in: float32 [4, 512, 512], P('groups', 'shard'), parts along dimension 0
- grad_group: float32 [4, 144, 512], P('groups', 'shard'), parts along dimension 0
- grad_out: float32 [4, 512, 512], P('groups', 'shard'), parts along dimension 0
The draws below stay inside these ranges and needn't reach their ends.
There are 2 independent parts, one for each index of `groups`. The reference program is written for one: setup_inputs(seed, part) draws one part's arguments, and reference() takes and returns one part's arrays. A program takes and returns all parts, laid end to end along the dimension named above; an argument that names none is the same for every part. Nothing has to cross between parts.
All inputs are finite; a program needn't handle non-finite values.
Results may differ from the reference program's by a relative error of at most 0.02.
Values may be sent and summed in bfloat16 or wider, within the bound.
A program may use at most 128 MiB of HBM per device.

```python
import math
import jax
import jax.numpy as jnp
from jax import lax

C = 512
GROUPS = 32
GW = 16
WIDTH = 512
BLOCKS = 2
H_DEV = 2
COLS = 128
TILES = 4
H = 8
PIXELS = 4096
N_ROWS = 4


def levels(own_key, shape, pieces, low, high):
    def one(axis_at, blocks):
        steps = jax.random.uniform(jax.random.fold_in(jax.random.fold_in(own_key, 6), axis_at), (blocks,), jnp.float32, low / len(pieces), high / len(pieces))
        return jnp.repeat(jnp.exp(steps), shape[axis_at] // blocks).reshape((-1,) + (1,) * (len(shape) - axis_at - 1))

    loudness = one(*pieces[0])
    for cut in pieces[1:]:
        loudness = loudness * one(*cut)
    return loudness


def noise(own_key, shape, spread, limit, split=(), dtype=jnp.bfloat16):
    loudness = levels(own_key, shape, split, -0.22, 0.18) if split else 1.0
    entries = jax.random.normal(own_key, shape, jnp.float32) * spread * loudness
    return jnp.minimum(jnp.maximum(entries, -limit), limit).astype(dtype)


def setup_inputs(seed: int = 0, part: int = 0) -> dict:
    arg_keys = jax.random.split(jax.random.key(seed), 6)
    own_keys = jax.random.split(jax.random.fold_in(arg_keys[5], part), 6)
    return {
        "images": noise(own_keys[0], (TILES, H, COLS, C), 1.0, 6.0, ((0, 4), (1, 4))),
        "cotangent": noise(own_keys[1], (TILES, H, COLS, C), 1.0, 6.0, ((0, 4), (1, 4))),
        "weight_in": noise(arg_keys[2], (BLOCKS, C, WIDTH), C ** -0.5, 0.25, ((1, 4),)),
        "weight_group": noise(arg_keys[3], (BLOCKS, 9 * GW, WIDTH), (9 * GW) ** -0.5, 0.5, ((1, 4),)),
        "weight_out": noise(arg_keys[4], (BLOCKS, WIDTH, C), WIDTH ** -0.5, 0.25, ((1, 4),)),
    }


def silu_slope(preact):
    sigmoid_value = jax.nn.sigmoid(preact)
    return sigmoid_value * (1.0 + preact * (1.0 - sigmoid_value))

def grouped_taps(padded, kernel, out_rows, out_cols, flipped, pattern):
    summed = None
    for tap_index in range(9):
        row_step = tap_index // 3
        col_step = tap_index % 3
        if flipped:
            row_step = 2 - row_step
            col_step = 2 - col_step
        window = padded[row_step:row_step + out_rows, col_step:col_step + out_cols, :]
        window = window.reshape(-1, GROUPS, GW).astype(jnp.float32)
        tap_term = jnp.einsum(pattern, window, kernel[tap_index].astype(jnp.float32))
        summed = tap_term if summed is None else summed + tap_term
    return summed

def rounded_sum(partials):
    rounded = lax.optimization_barrier(partials.astype(jnp.bfloat16))
    return lax.optimization_barrier(jnp.sum(rounded.astype(jnp.float32), axis=0))

def block_products(first_factor, second_factor):
    first_blocks = first_factor.reshape(N_ROWS, H_DEV * COLS, -1).astype(jnp.float32)
    second_blocks = second_factor.reshape(N_ROWS, H_DEV * COLS, -1).astype(jnp.float32)
    return rounded_sum(jnp.einsum('rpa,rpb->rab', first_blocks, second_blocks))

def tile_pass(images_tile, cotangent_tile, weight_in, weight_group, weight_out):
    height = H_DEV * N_ROWS
    pixels = height * COLS
    current = images_tile.reshape(pixels, C)
    stored = []
    for block_index in range(BLOCKS):
        kernel = weight_group[block_index].reshape(9, GW, GROUPS, GW)
        pre_one = jnp.dot(current, weight_in[block_index], preferred_element_type=jnp.float32)
        hidden_one = jax.nn.silu(pre_one).astype(jnp.bfloat16)
        padded_one = jnp.pad(hidden_one.reshape(height, COLS, WIDTH), ((1, 1), (1, 1), (0, 0)))
        pre_two = grouped_taps(padded_one, kernel, height, COLS, False, 'pgi,igo->pgo').reshape(pixels, WIDTH)
        hidden_two = jax.nn.silu(pre_two).astype(jnp.bfloat16)
        pre_three = current.astype(jnp.float32) + jnp.dot(hidden_two, weight_out[block_index], preferred_element_type=jnp.float32)
        stored.append((current, pre_one, padded_one, pre_two, hidden_two, pre_three, kernel))
        current = jax.nn.silu(pre_three).astype(jnp.bfloat16)
    decoded = current.reshape(height, COLS, C)
    grad_flow = cotangent_tile.reshape(pixels, C)
    grads_in = []
    grads_group = []
    grads_out = []
    for block_index in reversed(range(BLOCKS)):
        flow_in, pre_one, padded_one, pre_two, hidden_two, pre_three, kernel = stored[block_index]
        slope_three = grad_flow.astype(jnp.float32) * silu_slope(pre_three)
        low_three = slope_three.astype(jnp.bfloat16)
        grads_out.append(block_products(hidden_two, low_three))
        slope_two = (jnp.dot(low_three, weight_out[block_index].T, preferred_element_type=jnp.float32) * silu_slope(pre_two)).astype(jnp.bfloat16)
        slope_blocks = slope_two.reshape(N_ROWS, H_DEV * COLS, GROUPS, GW).astype(jnp.float32)
        tap_terms = []
        for tap_index in range(9):
            row_step = tap_index // 3
            col_step = tap_index % 3
            window = padded_one[row_step:row_step + height, col_step:col_step + COLS, :]
            window = window.reshape(N_ROWS, H_DEV * COLS, GROUPS, GW).astype(jnp.float32)
            tap_terms.append(rounded_sum(jnp.einsum('rpgi,rpgo->rigo', window, slope_blocks)))
        grads_group.append(jnp.stack(tap_terms).reshape(9 * GW, WIDTH))
        padded_slope = jnp.pad(slope_two.reshape(height, COLS, WIDTH), ((1, 1), (1, 1), (0, 0)))
        back_one = grouped_taps(padded_slope, kernel, height, COLS, True, 'pgo,igo->pgi').reshape(pixels, WIDTH)
        slope_one = (back_one * silu_slope(pre_one)).astype(jnp.bfloat16)
        grads_in.append(block_products(flow_in, slope_one))
        grad_flow = (slope_three + jnp.dot(slope_one, weight_in[block_index].T, preferred_element_type=jnp.float32)).astype(jnp.bfloat16)
    return (decoded, grad_flow.reshape(height, COLS, C), jnp.stack(grads_in[::-1]), jnp.stack(grads_group[::-1]), jnp.stack(grads_out[::-1]))

def reference(images, cotangent, weight_in, weight_group, weight_out):

    def one_tile(tile_pair):
        return tile_pass(tile_pair[0], tile_pair[1], weight_in, weight_group, weight_out)
    decoded, grad_images, tiles_in, tiles_group, tiles_out = lax.map(one_tile, (images, cotangent))
    norm_factor = 1.0 / math.sqrt(PIXELS)
    grad_in = lax.optimization_barrier(jnp.sum(tiles_in, axis=0)) * norm_factor
    grad_group = lax.optimization_barrier(jnp.sum(tiles_group, axis=0)) * norm_factor
    grad_out = lax.optimization_barrier(jnp.sum(tiles_out, axis=0)) * norm_factor
    return (decoded, grad_images, grad_in, grad_group, grad_out)
```

```python
import math

import jax
import jax.numpy as jnp
from jax import lax
from jax.sharding import PartitionSpec as P

GW = 16


def extended_2(cells, sides, width):
    for axis, dim in sides:
        count = lax.axis_size(axis)
        ends = count - 1
        head = lax.slice_in_dim(cells, 0, width, axis=dim)
        tail = lax.slice_in_dim(cells, cells.shape[dim] - width, cells.shape[dim], axis=dim)
        cells = jnp.concatenate(
            [
                lax.ppermute(tail, axis, [(i, (i + 1) % count) for i in range(ends)]),
                cells,
                lax.ppermute(head, axis, [((i + 1) % count, i) for i in range(ends)]),
            ],
            axis=dim,
        )
    return cells


def silu_slope(preact):
    sigmoid_value = jax.nn.sigmoid(preact)
    return sigmoid_value * (1.0 + preact * (1.0 - sigmoid_value))


def block_kernel(full_group, hidden_width, group_width):
    sub_width = min(hidden_width, 128)
    sections = hidden_width // sub_width
    members = sub_width // group_width
    arranged = full_group.reshape(9, group_width, sections, members, group_width)
    arranged = arranged.transpose(0, 2, 3, 1, 4)
    identity = jnp.eye(members, dtype=full_group.dtype)
    expanded = arranged[:, :, :, :, None, :] * identity[None, None, :, None, :, None]
    return expanded.reshape(9, sections, sub_width, sub_width)


def grouped_taps(padded, kernel, out_rows, out_cols, flipped, pattern):
    summed = None
    for tap_index in range(9):
        row_step = tap_index // 3
        col_step = tap_index % 3
        if flipped:
            row_step = 2 - row_step
            col_step = 2 - col_step
        window = padded[:, row_step : row_step + out_rows, col_step : col_step + out_cols, :]
        window = window.reshape(-1, kernel.shape[1], kernel.shape[2])
        tap_term = jnp.einsum(
            pattern, window, kernel[tap_index], preferred_element_type=jnp.float32
        )
        summed = tap_term if summed is None else summed + tap_term
    return summed


def body(images, cotangent, weight_in, weight_group, weight_out):
    tile_count, height, across, channels = images.shape
    block_count = weight_in.shape[0]
    group_width = GW
    pixels = tile_count * height * across
    current = images.reshape(pixels, channels)
    stored = []
    for block_index in range(block_count):
        full_in, full_group, full_out = (
            lax.all_gather(weight_in[block_index], "shard", axis=0, tiled=True),
            lax.all_gather(weight_group[block_index], "shard", axis=0, tiled=True),
            lax.all_gather(weight_out[block_index], "shard", axis=0, tiled=True),
        )
        hidden_width = full_in.shape[1]
        kernel = block_kernel(full_group, hidden_width, group_width)
        pre_one = jnp.dot(current, full_in, preferred_element_type=jnp.float32)
        hidden_one = (
            jax.nn.silu(pre_one)
            .astype(jnp.bfloat16)
            .reshape(tile_count, height, across, hidden_width)
        )
        haloed = extended_2(hidden_one, (("rows", 1),), 1)
        padded_one = jnp.pad(haloed, ((0, 0), (0, 0), (1, 1), (0, 0)))
        pre_two = grouped_taps(padded_one, kernel, height, across, False, "psi,sio->pso").reshape(
            pixels, hidden_width
        )
        hidden_two = jax.nn.silu(pre_two).astype(jnp.bfloat16)
        pre_three = current.astype(jnp.float32) + jnp.dot(
            hidden_two, full_out, preferred_element_type=jnp.float32
        )
        kept_weights = None
        stored.append((current, pre_one, padded_one, pre_two, hidden_two, pre_three, kept_weights))
        current = jax.nn.silu(pre_three).astype(jnp.bfloat16)
    decoded = current.reshape(images.shape)
    grad_flow = cotangent.reshape(pixels, channels)
    shares = []
    for block_index in reversed(range(block_count)):
        flow_in, pre_one, padded_one, pre_two, hidden_two, pre_three, kept_weights = stored[
            block_index
        ]
        full_in, full_group, full_out = (
            lax.all_gather(weight_in[block_index], "shard", axis=0, tiled=True),
            lax.all_gather(weight_group[block_index], "shard", axis=0, tiled=True),
            lax.all_gather(weight_out[block_index], "shard", axis=0, tiled=True),
        )
        hidden_width = full_in.shape[1]
        kernel = block_kernel(full_group, hidden_width, group_width)
        sections = kernel.shape[1]
        sub_width = kernel.shape[2]
        members = sub_width // group_width
        slope_three = grad_flow.astype(jnp.float32) * silu_slope(pre_three)
        low_three = slope_three.astype(jnp.bfloat16)
        part_out = jnp.einsum(
            "pw,pc->wc", hidden_two, low_three, preferred_element_type=jnp.float32
        )
        slope_two = (
            jnp.einsum("pc,wc->pw", low_three, full_out, preferred_element_type=jnp.float32)
            * silu_slope(pre_two)
        ).astype(jnp.bfloat16)
        slope_sections = slope_two.reshape(pixels, sections, sub_width)
        tap_terms = []
        for tap_index in range(9):
            row_step = tap_index // 3
            col_step = tap_index % 3
            window = padded_one[:, row_step : row_step + height, col_step : col_step + across, :]
            window = window.reshape(pixels, sections, sub_width)
            blockwise = jnp.einsum(
                "psi,pso->sio", window, slope_sections, preferred_element_type=jnp.float32
            )
            blockwise = blockwise.reshape(sections, members, group_width, members, group_width)
            same = jnp.eye(members, dtype=jnp.float32)[None, :, None, :, None]
            diagonal_part = jnp.sum(blockwise * same, axis=1)
            tap_terms.append(diagonal_part.transpose(1, 0, 2, 3).reshape(group_width, hidden_width))
        part_group = jnp.stack(tap_terms).reshape(9 * group_width, hidden_width)
        slope_grid = slope_two.reshape(tile_count, height, across, hidden_width)
        padded_slope = jnp.pad(slope_grid, ((0, 0), (2, 2), (1, 1), (0, 0)))
        extended = grouped_taps(padded_slope, kernel, height + 2, across, True, "pso,sio->psi")
        extended = extended.reshape(tile_count, height + 2, across, hidden_width)
        edge_rows = jnp.concatenate([extended[:, :1], extended[:, -1:]], axis=1)
        borders = extended_2(edge_rows.astype(jnp.bfloat16), (("rows", 1),), 1).astype(
            edge_rows.dtype
        )
        back_one = extended[:, 1:-1]
        back_one = back_one.at[:, :1].add(borders[:, :1])
        back_one = back_one.at[:, -1:].add(borders[:, -1:])
        slope_one = (back_one.reshape(pixels, hidden_width) * silu_slope(pre_one)).astype(
            jnp.bfloat16
        )
        part_in = jnp.einsum("pc,pw->cw", flow_in, slope_one, preferred_element_type=jnp.float32)
        grad_flow = (
            slope_three
            + jnp.einsum("pw,cw->pc", slope_one, full_in, preferred_element_type=jnp.float32)
        ).astype(jnp.bfloat16)
        shares.append(
            (
                lax.psum_scatter(
                    part_in.astype(jnp.bfloat16), "shard", scatter_dimension=0, tiled=True
                ).astype(jnp.float32),
                lax.psum_scatter(
                    part_group.astype(jnp.bfloat16), "shard", scatter_dimension=0, tiled=True
                ).astype(jnp.float32),
                lax.psum_scatter(
                    part_out.astype(jnp.bfloat16), "shard", scatter_dimension=0, tiled=True
                ).astype(jnp.float32),
            )
        )
    shares = shares[::-1]
    totals = (
        lax.psum(jnp.stack([entry[0] for entry in shares]).astype(jnp.bfloat16), "rows").astype(
            jnp.float32
        ),
        lax.psum(jnp.stack([entry[1] for entry in shares]).astype(jnp.bfloat16), "rows").astype(
            jnp.float32
        ),
        lax.psum(jnp.stack([entry[2] for entry in shares]).astype(jnp.bfloat16), "rows").astype(
            jnp.float32
        ),
    )
    norm_factor = 1.0 / math.sqrt(pixels * lax.axis_size("rows") * lax.axis_size("shard"))
    grad_images = grad_flow.reshape(images.shape)
    return (
        decoded,
        grad_images,
        totals[0] * norm_factor,
        totals[1] * norm_factor,
        totals[2] * norm_factor,
    )


def solution(mesh):
    placed = (
        P(("groups", "shard"), "rows", None, None),
        P(("groups", "shard"), "rows", None, None),
        P(None, "shard", None),
        P(None, "shard", None),
        P(None, "shard", None),
    )
    return jax.shard_map(
        body,
        mesh=mesh,
        in_specs=placed,
        out_specs=(
            P(("groups", "shard"), "rows", None, None),
            P(("groups", "shard"), "rows", None, None),
            P("groups", "shard", None),
            P("groups", "shard", None),
            P("groups", "shard", None),
        ),
        check_vma=False,
    )
```

```python
import functools
import math

import jax
import jax.numpy as jnp
from jax import lax
from jax.experimental import pallas as pl
from jax.experimental.pallas import tpu as pltpu
from jax.sharding import PartitionSpec as P

GW = 16
SEC = 256
F32 = jnp.float32
BF16 = jnp.bfloat16
MESH = pl.DeviceIdType.MESH


def bits_of(count):
    return [1 << k for k in range(count.bit_length() - 1)]


def up_to(value, step):
    return -(-value // step) * step


def dot(a, b, contract=((1,), (0,))):
    return lax.dot_general(a, b, (contract, ((), ())), preferred_element_type=F32)


def sigmoid(v):
    return 0.5 + 0.5 * jnp.tanh(0.5 * v)


class Links:
    def __init__(self, send_sems, recv_sems):
        self.send_sems, self.recv_sems = send_sems, recv_sems
        self.used = 0
        self.sent = []

    def copy(self, src, dst, axis, partner):
        k = self.used
        self.used += 1
        made = pltpu.make_async_remote_copy(
            src_ref=src,
            dst_ref=dst,
            send_sem=self.send_sems.at[k],
            recv_sem=self.recv_sems.at[k],
            device_id={axis: partner},
            device_id_type=MESH,
        )
        return made

    def start(self, src, dst, axis, partner):
        made = self.copy(src, dst, axis, partner)
        made.start()
        self.sent.append(made)
        return made


def other(me, bit):
    return me + bit * (1 - 2 * lax.rem(lax.div(me, bit), 2))


def gather_steps(links, buf, axis, me, count):
    for bit in reversed(bits_of(count)):
        copies = []
        for j in range(count // (2 * bit)):
            p = lax.rem(me, 2 * bit) + 2 * bit * j
            copies.append(links.start(buf.at[p], buf.at[p], axis, other(me, bit)))
        yield
        for c in copies:
            c.wait_recv()


def scatter_steps(links, buf, landing, axis, me, count):
    slot = 0
    for bit in bits_of(count):
        b = lax.rem(lax.div(me, bit), 2)
        copies = []
        for j in range(count // (2 * bit)):
            p = lax.rem(me, bit) + bit * (1 - b) + 2 * bit * j
            copies.append(links.start(buf.at[p], landing.at[slot + j], axis, other(me, bit)))
        yield
        for j, c in enumerate(copies):
            c.wait_recv()
            keep = lax.rem(me, bit) + bit * b + 2 * bit * j
            buf[keep] = (buf[keep].astype(F32) + landing[slot + j].astype(F32)).astype(BF16)
        slot += len(copies)


def kernel(n, rows, cols, norm, in_rows, *refs):
    (x_ref, cot_ref, wi_ref, wg_ref, wo_ref, dec_ref, gx_ref, gi_ref, gg_ref, go_ref,
     wi_full, wg_full, wo_full, wg_tmp, wg_flat, k_one, k_two, x3, y3, d1, d2, d3,
     h1, h2, a1, acc, sl3, low, sl2, sl1, halo, e1,
     p_in, p_out, p_group, group_tmp, l_in, l_out, l_group,
     q_in, q_out, q_group, lq_in, lq_out, lq_group, f_in, f_out, f_group,
     send_sems, recv_sems) = refs
    pixels = 2 * cols
    width = x_ref.shape[1]
    sections = width // SEC
    blocks = wi_ref.shape[0]
    grows = wg_ref.shape[1]
    me = lax.axis_index("shard")
    r = lax.axis_index("rows")
    has_up = jnp.where(r > 0, 1, 0)
    has_down = jnp.where(r < rows - 1, 1, 0)
    links = Links(send_sems, recv_sems)

    barrier = pltpu.get_barrier_semaphore()
    for bit in bits_of(n):
        pl.semaphore_signal(barrier, inc=1, device_id={"shard": other(me, bit)}, device_id_type=MESH)
    count = len(bits_of(n))
    if in_rows:
        for bit in bits_of(rows)[1:]:
            pl.semaphore_signal(barrier, inc=1, device_id={"rows": other(r, bit)}, device_id_type=MESH)
            count += 1

    @pl.when(r > 0)
    def _():
        pl.semaphore_signal(barrier, inc=1, device_id={"rows": lax.rem(r + rows - 1, rows)}, device_id_type=MESH)

    @pl.when(r < rows - 1)
    def _():
        pl.semaphore_signal(barrier, inc=1, device_id={"rows": lax.rem(r + 1, rows)}, device_id_type=MESH)

    for b in range(blocks):
        wi_full[b, me] = wi_ref[b]
        wo_full[b, me] = wo_ref[b]
        wg_tmp[...] = jnp.zeros_like(wg_tmp)
        wg_tmp[0:grows, :] = wg_ref[b].astype(F32)
        wg_full[b, me] = wg_tmp[...].astype(BF16)
    pl.semaphore_wait(barrier, count + has_up + has_down)

    gathers = []
    for b in range(blocks):
        for buf in (wi_full, wg_full, wo_full):
            gathers.append(gather_steps(links, buf.at[b], "shard", me, n))
    for g in gathers:
        next(g)

    def finish(g):
        for _ in g:
            pass

    def advance(gens):
        for g in list(gens):
            try:
                next(g)
            except StopIteration:
                gens.remove(g)

    col = lax.broadcasted_iota(jnp.int32, (cols, SEC), 0)
    first, last = col == 0, col == cols - 1
    mask = lax.broadcasted_iota(jnp.int32, (SEC, SEC), 0) // GW == lax.broadcasted_iota(jnp.int32, (SEC, SEC), 1) // GW

    def shifts(v):
        back = jnp.where(first, 0.0, pltpu.roll(v, 1, 0))
        ahead = jnp.where(last, 0.0, pltpu.roll(v, cols - 1, 0))
        return back, ahead

    def put(dst, sec, row, v, flipped):
        back, ahead = shifts(v)
        three = (ahead, v, back) if flipped else (back, v, ahead)
        for k in range(3):
            dst[sec, row * cols:(row + 1) * cols, k * SEC:(k + 1) * SEC] = three[k].astype(BF16)

    def halo_ends(at, src):
        up = pltpu.make_async_remote_copy(
            src_ref=src.at[pl.ds(0, cols)], dst_ref=halo.at[at, 1],
            send_sem=send_sems.at[base + 2 * at], recv_sem=recv_sems.at[base + 2 * at],
            device_id={"rows": lax.rem(r + rows - 1, rows)}, device_id_type=MESH)
        down = pltpu.make_async_remote_copy(
            src_ref=src.at[pl.ds(cols, cols)], dst_ref=halo.at[at, 0],
            send_sem=send_sems.at[base + 2 * at + 1], recv_sem=recv_sems.at[base + 2 * at + 1],
            device_id={"rows": lax.rem(r + 1, rows)}, device_id_type=MESH)
        return up, down

    total_gather = 3 * blocks * (n - 1)
    base = total_gather
    halo_sems = 4 * blocks

    def halo_send(at, src):
        @pl.when(r > 0)
        def _():
            halo_ends(at, src)[0].start()

        @pl.when(r < rows - 1)
        def _():
            halo_ends(at, src)[1].start()

    def halo_wait(at, src):
        @pl.when(r > 0)
        def _():
            up, down = halo_ends(at, src)
            down.wait_recv()
            up.wait_send()

        @pl.when(r == 0)
        def _():
            halo[at, 0] = jnp.zeros((cols, width), BF16)

        @pl.when(r < rows - 1)
        def _():
            up, down = halo_ends(at, src)
            up.wait_recv()
            down.wait_send()

        @pl.when(r == rows - 1)
        def _():
            halo[at, 1] = jnp.zeros((cols, width), BF16)

    def cut(s):
        return slice(s * SEC, (s + 1) * SEC)

    def expand(b):
        for p in range(n):
            wg_flat[p * grows:(p + 1) * grows, :] = wg_full[b, p].astype(F32)[:grows]
        for s in range(sections):
            for tap in range(9):
                dy, dx = tap // 3, tap % 3
                slab = wg_flat[tap * GW:(tap + 1) * GW, cut(s)]
                full = jnp.where(mask, jnp.concatenate([slab] * (SEC // GW), axis=0), 0.0).astype(BF16)
                k_one[b, s, dy, cut(dx), :] = full
                k_two[b, s, dy, :, cut(dx)] = full

    def forward(b, a_ref, out_ref):
        finish(gathers[3 * b])
        for s in range(sections):
            pre = dot(a_ref[...], wi_full[b, :, :, cut(s)].reshape(width, SEC))
            sg = sigmoid(pre)
            hid = pre * sg
            d1[b, :, cut(s)] = sg * (1.0 + pre * (1.0 - sg))
            h1[b, :, cut(s)] = hid.astype(BF16)
        halo_send(b, h1.at[b])
        if b == 0:
            for g in gathers[1:]:
                next(g, None)
        for s in range(sections):
            for row in range(2):
                put(x3.at[b], s, row + 1, h1[b, row * cols:(row + 1) * cols, cut(s)].astype(F32), False)
        finish(gathers[3 * b + 1])
        expand(b)
        for s in range(sections):
            acc[:, cut(s)] = dot(x3[b, s, cols:3 * cols, :], k_one[b, s, 1])
            acc[0:cols, cut(s)] += dot(x3[b, s, 2 * cols:3 * cols, :], k_one[b, s, 2])
            acc[cols:2 * cols, cut(s)] += dot(x3[b, s, cols:2 * cols, :], k_one[b, s, 0])
        halo_wait(b, h1.at[b])
        for s in range(sections):
            for side in range(2):
                put(x3.at[b], s, 3 * side, halo[b, side, :, cut(s)].astype(F32), False)
            top = acc[0:cols, cut(s)] + dot(x3[b, s, 0:cols, :], k_one[b, s, 0])
            low_ = acc[cols:2 * cols, cut(s)] + dot(x3[b, s, 3 * cols:4 * cols, :], k_one[b, s, 2])
            for row, pre in ((0, top), (1, low_)):
                at = slice(row * cols, (row + 1) * cols)
                sg = sigmoid(pre)
                d2[b, at, cut(s)] = sg * (1.0 + pre * (1.0 - sg))
                h2[b, at, cut(s)] = (pre * sg).astype(BF16)
        finish(gathers[3 * b + 2])
        for s in range(sections):
            pre = a_ref[:, cut(s)].astype(F32) + dot(h2[b], wo_full[b, :, :, cut(s)].reshape(width, SEC))
            sg = sigmoid(pre)
            d3[b, :, cut(s)] = sg * (1.0 + pre * (1.0 - sg))
            out_ref[:, cut(s)] = (pre * sg).astype(BF16)

    forward(0, x_ref, a1)
    forward(1, a1, dec_ref)
    links.used = total_gather + halo_sems

    live = []

    def reduce_steps(b, part, landing, q, landing_q, final, out):
        yield from scatter_steps(links, part.at[b], landing.at[b], "shard", me, n)
        if not in_rows:
            out[b] = part[b, me]
            return
        size = part.shape[2] // rows
        total = part[b, me]
        for k in range(rows):
            q[b, k] = total[k * size:(k + 1) * size]
        yield from scatter_steps(links, q.at[b], landing_q.at[b], "rows", r, rows)
        final[b, r] = q[b, r]
        yield from gather_steps(links, final.at[b], "rows", r, rows)
        out[b] = final[b].reshape(part.shape[2], width)[:out.shape[1]].astype(F32) * norm

    def launch(gen):
        live.append(gen)
        advance(live)

    def part_in(b, a_ref):
        for s in range(sections):
            made = dot(a_ref[...], sl1[:, cut(s)], ((0,), (0,))).astype(BF16)
            p_in[b, :, :, cut(s)] = made.reshape(n, width // n, SEC)
        launch(reduce_steps(b, p_in, l_in, q_in, lq_in, f_in, gi_ref))

    def backward(b, e_ref, a_ref, out_ref):
        for s in range(sections):
            v = e_ref[:, cut(s)].astype(F32) * d3[b, :, cut(s)]
            sl3[:, cut(s)] = v
            low[:, cut(s)] = v.astype(BF16)
        for s in range(sections):
            rows_of = wo_full[b].reshape(width, width)[cut(s), :]
            v = dot(low[...], rows_of, ((1,), (1,))) * d2[b, :, cut(s)]
            sl2[b, :, cut(s)] = v.astype(BF16)
        halo_send(blocks + b, sl2.at[b])
        for s in range(sections):
            made = dot(h2[b], low[:, cut(s)], ((0,), (0,))).astype(BF16)
            p_out[b, :, :, cut(s)] = made.reshape(n, width // n, SEC)
        launch(reduce_steps(b, p_out, l_out, q_out, lq_out, f_out, go_ref))
        for s in range(sections):
            for row in range(2):
                put(y3, s, row + 1, sl2[b, row * cols:(row + 1) * cols, cut(s)].astype(F32), True)
        for s in range(sections):
            acc[:, cut(s)] = dot(y3[s, cols:3 * cols, :], k_two[b, s, 1], ((1,), (1,)))
            acc[0:cols, cut(s)] += dot(y3[s, 2 * cols:3 * cols, :], k_two[b, s, 0], ((1,), (1,)))
            acc[cols:2 * cols, cut(s)] += dot(y3[s, cols:2 * cols, :], k_two[b, s, 2], ((1,), (1,)))
        halo_wait(blocks + b, sl2.at[b])
        advance(live)
        for s in range(sections):
            for side in range(2):
                put(y3, s, 3 * side, halo[blocks + b, side, :, cut(s)].astype(F32), True)
            top = acc[0:cols, cut(s)] + dot(y3[s, 0:cols, :], k_two[b, s, 2], ((1,), (1,)))
            low_ = acc[cols:2 * cols, cut(s)] + dot(y3[s, 3 * cols:4 * cols, :], k_two[b, s, 0], ((1,), (1,)))
            for row, back in ((0, top), (1, low_)):
                at = slice(row * cols, (row + 1) * cols)
                sl1[at, cut(s)] = (back * d1[b, at, cut(s)]).astype(BF16)
        part_in(b, a_ref)
        for s in range(sections):
            rows_of = wi_full[b].reshape(width, width)[cut(s), :]
            v = sl3[:, cut(s)] + dot(sl1[...], rows_of, ((1,), (1,)))
            out_ref[:, cut(s)] = v.astype(BF16)
        advance(live)
        for s in range(sections):
            for dy in range(3):
                made = dot(x3[b, s, dy * cols:(dy + 2) * cols, :], sl2[b, :, cut(s)], ((0,), (0,)))
                for dx in range(3):
                    tap = 3 * dy + dx
                    kept = jnp.where(mask, made[cut(dx), :], 0.0)
                    group_tmp[tap * GW:(tap + 1) * GW, cut(s)] = jnp.sum(kept.reshape(SEC // GW, GW, SEC), axis=0)
        gpad = p_group.shape[2]
        for p in range(n):
            p_group[b, p] = group_tmp[p * grows:p * grows + gpad, :].astype(BF16)
        launch(reduce_steps(b, p_group, l_group, q_group, lq_group, f_group, gg_ref))

    group_tmp[...] = jnp.zeros_like(group_tmp)
    backward(1, cot_ref, a1, e1)
    backward(0, e1, x_ref, gx_ref)
    while live:
        advance(live)
    for c in links.sent:
        c.wait_send()


def body(n, rows, images, cotangent, weight_in, weight_group, weight_out):
    tiles, height, cols, width = images.shape
    assert tiles == 1 and height == 2
    pixels = height * cols
    blocks, part, _ = weight_in.shape
    grows = weight_group.shape[1]
    wpad = up_to(grows, 16)
    in_rows = rows == 4 and part % (16 * rows) == 0
    gpad = up_to(grows, 16 * rows) if in_rows else wpad
    sections = width // SEC
    norm = 1.0 / math.sqrt(pixels * rows * n)
    out_type = F32 if in_rows else BF16
    gout = grows if in_rows else gpad
    qn = rows if in_rows else 1
    vm = pltpu.VMEM
    q, gq = part // qn, gpad // qn
    scratch = [
        vm((blocks, n, part, width), BF16), vm((blocks, n, wpad, width), BF16), vm((blocks, n, part, width), BF16),
        vm((wpad, width), F32), vm((up_to(n * grows, 16), width), F32),
        vm((blocks, sections, 3, 3 * SEC, SEC), BF16), vm((blocks, sections, 3, SEC, 3 * SEC), BF16),
        vm((blocks, sections, 4 * cols, 3 * SEC), BF16), vm((sections, 4 * cols, 3 * SEC), BF16),
        vm((blocks, pixels, width), F32), vm((blocks, pixels, width), F32), vm((blocks, pixels, width), F32),
        vm((blocks, pixels, width), BF16), vm((blocks, pixels, width), BF16), vm((pixels, width), BF16),
        vm((pixels, width), F32), vm((pixels, width), F32), vm((pixels, width), BF16),
        vm((blocks, pixels, width), BF16), vm((pixels, width), BF16),
        vm((2 * blocks, 2, cols, width), BF16), vm((pixels, width), BF16),
        vm((blocks, n, part, width), BF16), vm((blocks, n, part, width), BF16), vm((blocks, n, gpad, width), BF16),
        vm((up_to((n - 1) * grows + gpad, 16) + 16, width), F32),
        vm((blocks, n - 1, part, width), BF16), vm((blocks, n - 1, part, width), BF16), vm((blocks, n - 1, gpad, width), BF16),
        vm((blocks, qn, q, width), BF16), vm((blocks, qn, q, width), BF16), vm((blocks, qn, gq, width), BF16),
        vm((blocks, max(qn - 1, 1), q, width), BF16), vm((blocks, max(qn - 1, 1), q, width), BF16), vm((blocks, max(qn - 1, 1), gq, width), BF16),
        vm((blocks, qn, q, width), BF16), vm((blocks, qn, q, width), BF16), vm((blocks, qn, gq, width), BF16),
        pltpu.SemaphoreType.DMA((3 * blocks * (n - 1 + n - 1 + 2 * rows) + 4 * blocks if in_rows else 6 * blocks * (n - 1) + 4 * blocks,)),
        pltpu.SemaphoreType.DMA((3 * blocks * (n - 1 + n - 1 + 2 * rows) + 4 * blocks if in_rows else 6 * blocks * (n - 1) + 4 * blocks,)),
    ]
    spec = pl.BlockSpec(memory_space=pltpu.VMEM)
    dec, gx, gi, gg, go = pl.pallas_call(
        functools.partial(kernel, n, rows, cols, norm, in_rows),
        out_shape=[
            jax.ShapeDtypeStruct((pixels, width), BF16),
            jax.ShapeDtypeStruct((pixels, width), BF16),
            jax.ShapeDtypeStruct((blocks, part, width), out_type),
            jax.ShapeDtypeStruct((blocks, gout, width), out_type),
            jax.ShapeDtypeStruct((blocks, part, width), out_type),
        ],
        in_specs=[spec] * 5,
        out_specs=[spec] * 5,
        scratch_shapes=scratch,
        compiler_params=pltpu.CompilerParams(
            collective_id=0, has_side_effects=True, vmem_limit_bytes=58 * 2**20
        ),
    )(images.reshape(pixels, width), cotangent.reshape(pixels, width), weight_in, weight_group, weight_out)
    if not in_rows:
        gi, gg, go = (lax.psum(v, "rows").astype(F32) * norm for v in (gi, gg[:, :grows], go))
    return dec.reshape(images.shape), gx.reshape(images.shape), gi, gg, go


def solution(mesh):
    tile = P(("groups", "shard"), "rows", None, None)
    weight = P(None, "shard", None)
    grad = P("groups", "shard", None)
    return jax.shard_map(
        functools.partial(body, mesh.shape["shard"], mesh.shape["rows"]),
        mesh=mesh,
        in_specs=(tile, tile, weight, weight, weight),
        out_specs=(tile, tile, grad, grad, grad),
        check_vma=False,
    )
```

```python
import functools
import math

import jax
import jax.numpy as jnp
from jax import lax
from jax.experimental import pallas as pl
from jax.experimental.pallas import tpu as pltpu
from jax.sharding import PartitionSpec as P

GW = 16
SEC = 256
F32 = jnp.float32
BF16 = jnp.bfloat16
MESH = pl.DeviceIdType.MESH
STEPS = ((1, 2), (0, 0), (0, 2))


def bits_of(count):
    return [1 << k for k in range(count.bit_length() - 1)]


def up_to(value, step):
    return -(-value // step) * step


def dot(a, b, contract=((1,), (0,))):
    return lax.dot_general(a, b, (contract, ((), ())), preferred_element_type=F32)


def sigmoid(v):
    return 0.5 + 0.5 * jnp.tanh(0.5 * v)


class Links:
    def __init__(self, send_sems, recv_sems):
        self.send_sems, self.recv_sems = send_sems, recv_sems
        self.used = 0
        self.sent = []

    def copy(self, src, dst, axis, partner):
        k = self.used
        self.used += 1
        made = pltpu.make_async_remote_copy(
            src_ref=src,
            dst_ref=dst,
            send_sem=self.send_sems.at[k],
            recv_sem=self.recv_sems.at[k],
            device_id={axis: partner},
            device_id_type=MESH,
        )
        return made

    def start(self, src, dst, axis, partner):
        made = self.copy(src, dst, axis, partner)
        made.start()
        self.sent.append(made)
        return made


def other(me, bit):
    return me + bit * (1 - 2 * lax.rem(lax.div(me, bit), 2))


def gather_steps(links, buf, axis, me, count):
    for bit in reversed(bits_of(count)):
        copies = []
        for j in range(count // (2 * bit)):
            p = lax.rem(me, 2 * bit) + 2 * bit * j
            copies.append(links.start(buf.at[p], buf.at[p], axis, other(me, bit)))
        yield
        for c in copies:
            c.wait_recv()


def scatter_steps(links, buf, landing, axis, me, count):
    slot = 0
    for bit in bits_of(count):
        b = lax.rem(lax.div(me, bit), 2)
        copies = []
        for j in range(count // (2 * bit)):
            p = lax.rem(me, bit) + bit * (1 - b) + 2 * bit * j
            copies.append(links.start(buf.at[p], landing.at[slot + j], axis, other(me, bit)))
        yield
        for j, c in enumerate(copies):
            c.wait_recv()
            keep = lax.rem(me, bit) + bit * b + 2 * bit * j
            buf[keep] = (buf[keep].astype(F32) + landing[slot + j].astype(F32)).astype(BF16)
        slot += len(copies)


def kernel(n, rows, cols, norm, in_rows, *refs):
    (x_ref, cot_ref, wi_ref, wg_ref, wo_ref, dec_ref, gx_ref, gi_ref, gg_ref, go_ref,
     wi_full, wg_full, wo_full, wg_tmp, wg_flat, k_one, k_two, x3, y3, d1, d2, d3,
     h1, h2, a1, acc, sl3, low, sl2, sl1, halo, e1,
     p_in, p_out, p_group, group_tmp, l_in, l_out, l_group,
     q_in, q_out, q_group, lq_in, lq_out, lq_group, f_in, f_out, f_group,
     send_sems, recv_sems) = refs
    pixels = 2 * cols
    width = x_ref.shape[1]
    sections = width // SEC
    blocks = wi_ref.shape[0]
    grows = wg_ref.shape[0]
    me = lax.axis_index("shard")
    r = lax.axis_index("rows")
    has_up = jnp.where(r > 0, 1, 0)
    has_down = jnp.where(r < rows - 1, 1, 0)
    links = Links(send_sems, recv_sems)

    barrier = pltpu.get_barrier_semaphore()
    for bit in bits_of(n):
        pl.semaphore_signal(barrier, inc=1, device_id={"shard": other(me, bit)}, device_id_type=MESH)
    count = len(bits_of(n))
    if in_rows:
        for bit in bits_of(rows)[1:]:
            pl.semaphore_signal(barrier, inc=1, device_id={"rows": other(r, bit)}, device_id_type=MESH)
            count += 1

    @pl.when(r > 0)
    def _():
        pl.semaphore_signal(barrier, inc=1, device_id={"rows": lax.rem(r + rows - 1, rows)}, device_id_type=MESH)

    @pl.when(r < rows - 1)
    def _():
        pl.semaphore_signal(barrier, inc=1, device_id={"rows": lax.rem(r + 1, rows)}, device_id_type=MESH)

    for b in range(blocks):
        wi_full[b, me] = wi_ref[b]
        wo_full[b, me] = wo_ref[b]
        wg_tmp[...] = jnp.zeros_like(wg_tmp)
        wg_tmp[0:grows, :] = wg_ref[...].astype(F32)[:, b, :]
        wg_full[b, me] = wg_tmp[...].astype(BF16)
    pl.semaphore_wait(barrier, count + has_up + has_down)

    gathers = []
    for b in range(blocks):
        for buf in (wi_full, wg_full, wo_full):
            gathers.append(gather_steps(links, buf.at[b], "shard", me, n))
    for g in gathers:
        next(g)

    def finish(g):
        for _ in g:
            pass

    def advance(gens):
        for g in list(gens):
            try:
                next(g)
            except StopIteration:
                gens.remove(g)

    col = lax.broadcasted_iota(jnp.int32, (cols, SEC), 0)
    first, last = col == 0, col == cols - 1
    mask = lax.broadcasted_iota(jnp.int32, (SEC, SEC), 0) // GW == lax.broadcasted_iota(jnp.int32, (SEC, SEC), 1) // GW

    def shifts(v):
        back = jnp.where(first, 0.0, pltpu.roll(v, 1, 0))
        ahead = jnp.where(last, 0.0, pltpu.roll(v, cols - 1, 0))
        return back, ahead

    def put(dst, sec, row, v, flipped):
        back, ahead = shifts(v)
        three = (ahead, v, back) if flipped else (back, v, ahead)
        for k in range(3):
            dst[sec, row * cols:(row + 1) * cols, k * SEC:(k + 1) * SEC] = three[k].astype(BF16)

    def halo_ends(at, src):
        up = pltpu.make_async_remote_copy(
            src_ref=src.at[pl.ds(0, cols)], dst_ref=halo.at[at, 1],
            send_sem=send_sems.at[base + 2 * at], recv_sem=recv_sems.at[base + 2 * at],
            device_id={"rows": lax.rem(r + rows - 1, rows)}, device_id_type=MESH)
        down = pltpu.make_async_remote_copy(
            src_ref=src.at[pl.ds(cols, cols)], dst_ref=halo.at[at, 0],
            send_sem=send_sems.at[base + 2 * at + 1], recv_sem=recv_sems.at[base + 2 * at + 1],
            device_id={"rows": lax.rem(r + 1, rows)}, device_id_type=MESH)
        return up, down

    total_gather = 3 * blocks * (n - 1)
    base = total_gather
    halo_sems = 4 * blocks

    def halo_send(at, src):
        @pl.when(r > 0)
        def _():
            halo_ends(at, src)[0].start()

        @pl.when(r < rows - 1)
        def _():
            halo_ends(at, src)[1].start()

    def halo_wait(at, src):
        @pl.when(r > 0)
        def _():
            up, down = halo_ends(at, src)
            down.wait_recv()
            up.wait_send()

        @pl.when(r == 0)
        def _():
            halo[at, 0] = jnp.zeros((cols, width), BF16)

        @pl.when(r < rows - 1)
        def _():
            up, down = halo_ends(at, src)
            up.wait_recv()
            down.wait_send()

        @pl.when(r == rows - 1)
        def _():
            halo[at, 1] = jnp.zeros((cols, width), BF16)

    def cut(s):
        return slice(s * SEC, (s + 1) * SEC)

    def expand(b):
        for p in range(n):
            wg_flat[p * grows:(p + 1) * grows, :] = wg_full[b, p].astype(F32)[:grows]
        for s in range(sections):
            for tap in range(9):
                dy, dx = tap // 3, tap % 3
                slab = wg_flat[tap * GW:(tap + 1) * GW, cut(s)]
                full = jnp.where(mask, jnp.concatenate([slab] * (SEC // GW), axis=0), 0.0).astype(BF16)
                k_one[b, s, dy, cut(dx), :] = full
                k_two[b, s, dy, :, cut(dx)] = full

    def forward(b, a_ref, out_ref):
        finish(gathers[3 * b])
        for s in range(sections):
            pre = dot(a_ref[...], wi_full[b, :, :, cut(s)].reshape(width, SEC))
            sg = sigmoid(pre)
            hid = pre * sg
            d1[b, :, cut(s)] = sg * (1.0 + pre * (1.0 - sg))
            h1[b, :, cut(s)] = hid.astype(BF16)
        halo_send(b, h1.at[b])
        for s in range(sections):
            for row in range(2):
                put(x3.at[b], s, row + 1, h1[b, row * cols:(row + 1) * cols, cut(s)].astype(F32), False)
        finish(gathers[3 * b + 1])
        next(gathers[3 * b + 2], None)
        expand(b)
        for s in range(sections):
            acc[:, cut(s)] = dot(x3[b, s, cols:3 * cols, :], k_one[b, s, 1])
            acc[0:cols, cut(s)] += dot(x3[b, s, 2 * cols:3 * cols, :], k_one[b, s, 2])
            acc[cols:2 * cols, cut(s)] += dot(x3[b, s, cols:2 * cols, :], k_one[b, s, 0])
        halo_wait(b, h1.at[b])
        for s in range(sections):
            for side in range(2):
                put(x3.at[b], s, 3 * side, halo[b, side, :, cut(s)].astype(F32), False)
            top = acc[0:cols, cut(s)] + dot(x3[b, s, 0:cols, :], k_one[b, s, 0])
            low_ = acc[cols:2 * cols, cut(s)] + dot(x3[b, s, 3 * cols:4 * cols, :], k_one[b, s, 2])
            for row, pre in ((0, top), (1, low_)):
                at = slice(row * cols, (row + 1) * cols)
                sg = sigmoid(pre)
                d2[b, at, cut(s)] = sg * (1.0 + pre * (1.0 - sg))
                h2[b, at, cut(s)] = (pre * sg).astype(BF16)
        finish(gathers[3 * b + 2])
        if b + 1 < blocks:
            next(gathers[3 * b + 3], None)
        for s in range(sections):
            pre = a_ref[:, cut(s)].astype(F32) + dot(h2[b], wo_full[b, :, :, cut(s)].reshape(width, SEC))
            sg = sigmoid(pre)
            d3[b, :, cut(s)] = sg * (1.0 + pre * (1.0 - sg))
            out_ref[:, cut(s)] = (pre * sg).astype(BF16)

    forward(0, x_ref, a1)
    forward(1, a1, dec_ref)
    links.used = total_gather + halo_sems

    live = []

    def reduce_steps(b, part, landing, q, landing_q, final, out):
        yield from scatter_steps(links, part.at[b], landing.at[b], "shard", me, n)
        if not in_rows:
            out[b] = part[b, me]
            return
        size = part.shape[2] // rows
        total = part[b, me]
        for k in range(rows):
            q[b, k] = total[k * size:(k + 1) * size]
        yield from scatter_steps(links, q.at[b], landing_q.at[b], "rows", r, rows)
        final[b, r] = q[b, r]
        yield from gather_steps(links, final.at[b], "rows", r, rows)
        done = final[b].reshape(part.shape[2], width).astype(F32) * norm
        if out is gg_ref:
            out[:, b, :] = done[:grows]
        else:
            out[b] = done

    def launch(gen):
        next(gen)
        live.append(gen)

    def step_at(b, at):
        if (b, at) in STEPS:
            advance(live)

    def part_in(b, a_ref):
        for s in range(sections):
            made = dot(a_ref[...], sl1[:, cut(s)], ((0,), (0,))).astype(BF16)
            p_in[b, :, :, cut(s)] = made.reshape(n, width // n, SEC)
        launch(reduce_steps(b, p_in, l_in, q_in, lq_in, f_in, gi_ref))

    def backward(b, e_ref, a_ref, out_ref):
        for s in range(sections):
            v = e_ref[:, cut(s)].astype(F32) * d3[b, :, cut(s)]
            sl3[:, cut(s)] = v
            low[:, cut(s)] = v.astype(BF16)
        for s in range(sections):
            rows_of = wo_full[b].reshape(width, width)[cut(s), :]
            v = dot(low[...], rows_of, ((1,), (1,))) * d2[b, :, cut(s)]
            sl2[b, :, cut(s)] = v.astype(BF16)
        halo_send(blocks + b, sl2.at[b])
        for s in range(sections):
            made = dot(h2[b], low[:, cut(s)], ((0,), (0,))).astype(BF16)
            p_out[b, :, :, cut(s)] = made.reshape(n, width // n, SEC)
        launch(reduce_steps(b, p_out, l_out, q_out, lq_out, f_out, go_ref))
        for s in range(sections):
            for row in range(2):
                put(y3, s, row + 1, sl2[b, row * cols:(row + 1) * cols, cut(s)].astype(F32), True)
        for s in range(sections):
            acc[:, cut(s)] = dot(y3[s, cols:3 * cols, :], k_two[b, s, 1], ((1,), (1,)))
            acc[0:cols, cut(s)] += dot(y3[s, 2 * cols:3 * cols, :], k_two[b, s, 0], ((1,), (1,)))
            acc[cols:2 * cols, cut(s)] += dot(y3[s, cols:2 * cols, :], k_two[b, s, 2], ((1,), (1,)))
        step_at(b, 0)
        for s in range(sections):
            for dy in range(3):
                made = dot(x3[b, s, dy * cols:(dy + 2) * cols, :], sl2[b, :, cut(s)], ((0,), (0,)))
                for dx in range(3):
                    tap = 3 * dy + dx
                    kept = jnp.where(mask, made[cut(dx), :], 0.0)
                    group_tmp[tap * GW:(tap + 1) * GW, cut(s)] = jnp.sum(kept.reshape(SEC // GW, GW, SEC), axis=0)
        gpad = p_group.shape[2]
        for p in range(n):
            p_group[b, p] = group_tmp[p * grows:p * grows + gpad, :].astype(BF16)
        launch(reduce_steps(b, p_group, l_group, q_group, lq_group, f_group, gg_ref))
        step_at(b, 1)
        halo_wait(blocks + b, sl2.at[b])
        step_at(b, 2)
        for s in range(sections):
            for side in range(2):
                put(y3, s, 3 * side, halo[blocks + b, side, :, cut(s)].astype(F32), True)
            top = acc[0:cols, cut(s)] + dot(y3[s, 0:cols, :], k_two[b, s, 2], ((1,), (1,)))
            low_ = acc[cols:2 * cols, cut(s)] + dot(y3[s, 3 * cols:4 * cols, :], k_two[b, s, 0], ((1,), (1,)))
            for row, back in ((0, top), (1, low_)):
                at = slice(row * cols, (row + 1) * cols)
                sl1[at, cut(s)] = (back * d1[b, at, cut(s)]).astype(BF16)
        def flow():
            for s in range(sections):
                rows_of = wi_full[b].reshape(width, width)[cut(s), :]
                v = sl3[:, cut(s)] + dot(sl1[...], rows_of, ((1,), (1,)))
                out_ref[:, cut(s)] = v.astype(BF16)

        part_in(b, a_ref)
        step_at(b, 3)
        flow()
        step_at(b, 4)

    group_tmp[...] = jnp.zeros_like(group_tmp)
    backward(1, cot_ref, a1, e1)
    backward(0, e1, x_ref, gx_ref)
    while live:
        advance(live)
    for c in links.sent:
        c.wait_send()


def body(n, rows, images, cotangent, weight_in, weight_group, weight_out):
    tiles, height, cols, width = images.shape
    assert tiles == 1 and height == 2
    pixels = height * cols
    blocks, part, _ = weight_in.shape
    grows = weight_group.shape[1]
    wpad = up_to(grows, 16)
    in_rows = rows == 4 and part % (16 * rows) == 0
    gpad = up_to(grows, 16 * rows) if in_rows else wpad
    sections = width // SEC
    norm = 1.0 / math.sqrt(pixels * rows * n)
    out_type = F32 if in_rows else BF16
    gout = grows if in_rows else gpad
    qn = rows if in_rows else 1
    vm = pltpu.VMEM
    q, gq = part // qn, gpad // qn
    scratch = [
        vm((blocks, n, part, width), BF16), vm((blocks, n, wpad, width), BF16), vm((blocks, n, part, width), BF16),
        vm((wpad, width), F32), vm((up_to(n * grows, 16), width), F32),
        vm((blocks, sections, 3, 3 * SEC, SEC), BF16), vm((blocks, sections, 3, SEC, 3 * SEC), BF16),
        vm((blocks, sections, 4 * cols, 3 * SEC), BF16), vm((sections, 4 * cols, 3 * SEC), BF16),
        vm((blocks, pixels, width), F32), vm((blocks, pixels, width), F32), vm((blocks, pixels, width), F32),
        vm((blocks, pixels, width), BF16), vm((blocks, pixels, width), BF16), vm((pixels, width), BF16),
        vm((pixels, width), F32), vm((pixels, width), F32), vm((pixels, width), BF16),
        vm((blocks, pixels, width), BF16), vm((pixels, width), BF16),
        vm((2 * blocks, 2, cols, width), BF16), vm((pixels, width), BF16),
        vm((blocks, n, part, width), BF16), vm((blocks, n, part, width), BF16), vm((blocks, n, gpad, width), BF16),
        vm((up_to((n - 1) * grows + gpad, 16) + 16, width), F32),
        vm((blocks, n - 1, part, width), BF16), vm((blocks, n - 1, part, width), BF16), vm((blocks, n - 1, gpad, width), BF16),
        vm((blocks, qn, q, width), BF16), vm((blocks, qn, q, width), BF16), vm((blocks, qn, gq, width), BF16),
        vm((blocks, max(qn - 1, 1), q, width), BF16), vm((blocks, max(qn - 1, 1), q, width), BF16), vm((blocks, max(qn - 1, 1), gq, width), BF16),
        vm((blocks, qn, q, width), BF16), vm((blocks, qn, q, width), BF16), vm((blocks, qn, gq, width), BF16),
        pltpu.SemaphoreType.DMA((3 * blocks * (n - 1 + n - 1 + 2 * rows) + 4 * blocks if in_rows else 6 * blocks * (n - 1) + 4 * blocks,)),
        pltpu.SemaphoreType.DMA((3 * blocks * (n - 1 + n - 1 + 2 * rows) + 4 * blocks if in_rows else 6 * blocks * (n - 1) + 4 * blocks,)),
    ]
    spec = pl.BlockSpec(memory_space=pltpu.VMEM)
    dec, gx, gi, gg, go = pl.pallas_call(
        functools.partial(kernel, n, rows, cols, norm, in_rows),
        out_shape=[
            jax.ShapeDtypeStruct((pixels, width), BF16),
            jax.ShapeDtypeStruct((pixels, width), BF16),
            jax.ShapeDtypeStruct((blocks, part, width), out_type),
            jax.ShapeDtypeStruct((grows, blocks, width) if in_rows else (blocks, gout, width), out_type),
            jax.ShapeDtypeStruct((blocks, part, width), out_type),
        ],
        in_specs=[spec] * 5,
        out_specs=[spec] * 5,
        scratch_shapes=scratch,
        compiler_params=pltpu.CompilerParams(
            collective_id=0, has_side_effects=True, vmem_limit_bytes=58 * 2**20
        ),
    )(images.reshape(pixels, width), cotangent.reshape(pixels, width), weight_in, weight_group.transpose(1, 0, 2), weight_out)
    if in_rows:
        gg = gg.transpose(1, 0, 2)
    else:
        gi, gg, go = (lax.psum(v, "rows").astype(F32) * norm for v in (gi, gg[:, :grows], go))
    return dec.reshape(images.shape), gx.reshape(images.shape), gi, gg, go


def solution(mesh):
    tile = P(("groups", "shard"), "rows", None, None)
    weight = P(None, "shard", None)
    grad = P("groups", "shard", None)
    return jax.shard_map(
        functools.partial(body, mesh.shape["shard"], mesh.shape["rows"]),
        mesh=mesh,
        in_specs=(tile, tile, weight, weight, weight),
        out_specs=(tile, tile, grad, grad, grad),
        check_vma=False,
    )
```
